32 devices in a mesh: pop: 8 (over z, x), tensor: 4 (over y, core).
Axes of the slice: x: 2, y: 2, z: 4, core: 2. Of those that a mesh axis runs over, the one named last changes fastest.
Arguments:
- token_ids: int32 [64, 64], P('pop'), may hold values from 0 to 76031, as said below
- ranks: int32 [64], P('pop'), may hold values from 0 to 63, each once
- embed_table: bfloat16 [76032, 3584], P('pop', 'tensor'), may hold values from -6 to 6
- norm_gain: bfloat16 [3584], replicated, may hold values from 0.5 to 1.5
- gate_weight: bfloat16 [3584, 18944], P('pop', 'tensor'), may hold values from -0.09375 to 0.09375
- up_weight: bfloat16 [3584, 18944], P('pop', 'tensor'), may hold values from -0.09375 to 0.09375
- gate_left: bfloat16 [64, 3584], P('pop'), may hold values from -6 to 6
- up_left: bfloat16 [64, 3584], P('pop'), may hold values from -6 to 6
- gate_right: bfloat16 [64, 18944], P('pop', 'tensor'), may hold values from -6 to 6
- up_right: bfloat16 [64, 18944], P('pop', 'tensor'), may hold values from -6 to 6
Outputs:
- hidden: bfloat16 [4096, 18944], P('pop', 'tensor')
- gate_step: float32 [3584, 18944], P('pop', 'tensor')
- up_step: float32 [3584, 18944], P('pop', 'tensor')
The draws below stay inside these ranges and needn't reach their ends.
Inputs may be any that keep to these rules, and one draw needn't show every extreme that they name: Split token_ids into aligned blocks of 8 members (the members of one index of pop) and the table into blocks of 9504 rows: in every block of members, at most 128 ids fall in any one block of table rows, and exactly 128 in one of them.
All inputs are finite; a program needn't handle non-finite values.
Results may differ from the reference program's by a relative error of at most 0.0058.
Values may be sent and summed in bfloat16 or wider, within the bound.
A program may use at most 256 MiB of HBM per device.

```python
import math
import jax
import jax.numpy as jnp
from jax import lax

D = 3584
FF = 18944
VOCAB = 76032
PROMPT = 64
MEM_DEV = 8
MEMBERS = 64
TABLE_SHARD = 9504
ID_CAP = 128


def draw_token_ids(key, part):
    block = MEM_DEV * PROMPT
    owners = VOCAB // TABLE_SHARD
    count = MEMBERS * PROMPT // block

    def one_block(block_key):
        key_hot, key_off, key_order, key_row = jax.random.split(block_key, 4)
        hot = jax.random.randint(key_hot, (), 0, owners)
        offset = jax.random.randint(key_off, (), 0, owners - 1)
        index = jnp.arange(block, dtype=jnp.int32)
        other = (hot + 1 + (index + offset) % (owners - 1)) % owners
        owner = jnp.where(index < ID_CAP, hot, other)
        order = jax.random.permutation(key_order, block)
        owner = owner[order]
        row = jax.random.randint(key_row, (block,), 0, TABLE_SHARD)
        return (owner * TABLE_SHARD + row).astype(jnp.int32)
    keys = jax.random.split(jax.random.fold_in(key, 7), count)
    return jax.vmap(one_block)(keys).reshape(MEMBERS, PROMPT).astype(jnp.int32)


def shard_levels(key, extent, pieces, least, high):
    factor_of = 1.0
    for position, shards_of in pieces:
        draws = jax.random.uniform(jax.random.fold_in(jax.random.fold_in(key, 6), position), (shards_of,), jnp.float32, least / len(pieces), high / len(pieces))
        factor_of = factor_of * jnp.repeat(jnp.exp(draws), extent[position] // shards_of).reshape((-1,) + (1,) * (len(extent) - 1 - position))
    return factor_of


def noise(key, extent, spread, limit, shards=(), kind=jnp.bfloat16):
    array = spread * jax.random.normal(key, extent, jnp.float32)
    if shards:
        array = array * shard_levels(key, extent, shards, -0.22, 0.18)
    return jnp.clip(array, -limit, limit).astype(kind)


def setup_inputs(seed: int = 0) -> dict:
    key_of = jax.random.split(jax.random.key(seed), 11)
    return {
        "token_ids": draw_token_ids(jax.random.fold_in(key_of[10], 71), 0),
        "ranks": jax.random.permutation(key_of[1], MEMBERS).astype(jnp.int32),
        "embed_table": noise(key_of[2], (VOCAB, D), 1.0, 6.0, ((0, 8), (1, 4))),
        "norm_gain": jnp.clip(1.0 + 0.1 * jax.random.normal(key_of[3], (D,), jnp.float32), 0.5, 1.5).astype(jnp.bfloat16),
        "gate_weight": noise(key_of[4], (D, FF), D ** -0.5, 0.09375, ((0, 8), (1, 4))),
        "up_weight": noise(key_of[5], (D, FF), D ** -0.5, 0.09375, ((0, 8), (1, 4))),
        "gate_left": noise(key_of[6], (MEMBERS, D), 1.0, 6.0, ((0, 8),)),
        "up_left": noise(key_of[7], (MEMBERS, D), 1.0, 6.0, ((0, 8),)),
        "gate_right": noise(key_of[8], (MEMBERS, FF), 1.0, 6.0, ((0, 8), (1, 4))),
        "up_right": noise(key_of[9], (MEMBERS, FF), 1.0, 6.0, ((0, 8), (1, 4))),
    }


def reference(token_ids, ranks, embed_table, norm_gain, gate_weight, up_weight, gate_left, up_left, gate_right, up_right):
    embedded = embed_table[token_ids.reshape(-1)]
    values = embedded.astype(jnp.float32)
    meansq = lax.optimization_barrier(jnp.mean(values * values, axis=-1, keepdims=True))
    normed = (values * lax.rsqrt(meansq + 1e-06) * norm_gain.astype(jnp.float32)).astype(jnp.bfloat16)
    blocks = normed.reshape(MEMBERS, PROMPT, D)
    scale = 1.0 / math.sqrt(D)

    def member(items):
        rows, left_gate, left_up, right_gate, right_up = items
        gate_base = jnp.dot(rows, gate_weight, preferred_element_type=jnp.float32)
        up_base = jnp.dot(rows, up_weight, preferred_element_type=jnp.float32)
        gate_side = jnp.dot(rows, left_gate, preferred_element_type=jnp.float32) * scale
        up_side = jnp.dot(rows, left_up, preferred_element_type=jnp.float32) * scale
        gate = gate_base + 0.5 * gate_side[:, None] * right_gate.astype(jnp.float32)[None, :]
        up = up_base + 0.5 * up_side[:, None] * right_up.astype(jnp.float32)[None, :]
        return (jax.nn.silu(gate) * up).astype(jnp.bfloat16)
    hidden = lax.map(member, (blocks, gate_left, up_left, gate_right, up_right)).reshape(MEMBERS * PROMPT, FF)
    score = (2.0 * ranks.astype(jnp.float32) - (MEMBERS - 1)) / (MEMBERS - 1)
    norm_count = 1.0 / math.sqrt(MEMBERS)
    gate_step = jnp.dot((gate_left.astype(jnp.float32) * score[:, None]).T, gate_right.astype(jnp.float32), precision=lax.Precision.HIGHEST) * norm_count
    up_step = jnp.dot((up_left.astype(jnp.float32) * score[:, None]).T, up_right.astype(jnp.float32), precision=lax.Precision.HIGHEST) * norm_count
    return (hidden, gate_step, up_step)
```

```python
import math

import jax
import jax.numpy as jnp
from jax import lax
from jax.sharding import PartitionSpec as P


def split_high(x):
    high = lax.reduce_precision(x, exponent_bits=8, mantissa_bits=7)
    low = x - high
    return jnp.concatenate([high.astype(jnp.bfloat16), low.astype(jnp.bfloat16)], axis=0)


def weighted_step(left, right, score):
    scaled = split_high(left.astype(jnp.float32) * score[:, None])
    both = jnp.concatenate([right, right], axis=0)
    return lax.dot_general(
        scaled, both, (((0,), (0,)), ((), ())), preferred_element_type=jnp.float32
    )


def per_device(
    token_ids,
    ranks,
    embed_table,
    norm_gain,
    gate_weight,
    up_weight,
    gate_left,
    up_left,
    gate_right,
    up_right,
):
    pops = lax.axis_size("pop")
    pop = lax.axis_index("pop")
    tensor = lax.axis_index("tensor")
    table_rows, features = embed_table.shape
    own_members, prompt = token_ids.shape
    row_count, hidden_cols = gate_weight.shape
    width = norm_gain.shape[0]
    members = own_members * pops
    part = -(-hidden_cols // (128 * pops)) * 128
    padded = part * pops

    def pad_cols(x):
        return jnp.pad(x, ((0, 0), (0, padded - hidden_cols)))

    all_ids = lax.all_gather(token_ids, "pop", axis=0, tiled=True)
    all_ranks = lax.all_gather(ranks, "pop", axis=0, tiled=True)
    local_ids = all_ids.reshape(-1) - pop * table_rows
    owned = (local_ids >= 0) & (local_ids < table_rows)
    picked = jnp.take(embed_table, jnp.clip(local_ids, 0, table_rows - 1), axis=0)
    partial_rows = jnp.where(owned[:, None], picked, jnp.bfloat16(0))
    own_cols = lax.psum_scatter(partial_rows, "pop", scatter_dimension=0, tiled=True)

    gate_cols = lax.all_to_all(pad_cols(gate_weight), "pop", 1, 0, tiled=True)
    up_cols = lax.all_to_all(pad_cols(up_weight), "pop", 1, 0, tiled=True)

    values = own_cols.astype(jnp.float32)
    total = lax.psum(jnp.sum(values * values, axis=-1), "tensor")
    gain = lax.dynamic_slice_in_dim(norm_gain, tensor * features, features, 0)
    own_normed = (
        values * lax.rsqrt(total[:, None] * (1.0 / width) + 1e-06) * gain.astype(jnp.float32)
    ).astype(jnp.bfloat16)
    some = lax.all_gather(own_normed, "pop", axis=0, tiled=True)
    normed = lax.all_gather(some, "tensor", axis=1, tiled=True)

    all_gl, all_ul, all_gr, all_ur = (
        lax.all_gather(gate_left, "pop", axis=0, tiled=True),
        lax.all_gather(up_left, "pop", axis=0, tiled=True),
        lax.all_gather(gate_right, "pop", axis=0, tiled=True),
        lax.all_gather(up_right, "pop", axis=0, tiled=True),
    )
    scale = 0.5 / math.sqrt(width)
    blocks = normed.reshape(members, prompt, width)

    def project(weight, left, right):
        base = jnp.dot(normed, weight, preferred_element_type=jnp.float32)
        side = jnp.einsum("mld,md->ml", blocks, left, preferred_element_type=jnp.float32) * scale
        cols = lax.dynamic_slice_in_dim(pad_cols(right), pop * part, part, 1)
        return (
            base.reshape(members, prompt, part)
            + side[:, :, None] * cols.astype(jnp.float32)[:, None, :]
        )

    gate = project(gate_cols, all_gl, all_gr)
    up = project(up_cols, all_ul, all_ur)
    mine = (jax.nn.silu(gate) * up).astype(jnp.bfloat16).reshape(members * prompt, part)
    hidden = lax.all_to_all(mine, "pop", 0, 1, tiled=True)[:, :hidden_cols]

    score = (2.0 * all_ranks.astype(jnp.float32) - (members - 1)) / (members - 1)
    score = score * (1.0 / math.sqrt(members))
    row_start = pop * row_count
    left_gate = lax.dynamic_slice_in_dim(all_gl, row_start, row_count, 1)
    left_up = lax.dynamic_slice_in_dim(all_ul, row_start, row_count, 1)
    gate_step = weighted_step(left_gate, all_gr, score)
    up_step = weighted_step(left_up, all_ur, score)
    return (hidden, gate_step, up_step)


def solution(mesh):
    in_specs = (
        P("pop", None),
        P("pop"),
        P("pop", "tensor"),
        P(),
        P("pop", "tensor"),
        P("pop", "tensor"),
        P("pop", None),
        P("pop", None),
        P("pop", "tensor"),
        P("pop", "tensor"),
    )
    out_specs = (P("pop", "tensor"), P("pop", "tensor"), P("pop", "tensor"))
    return jax.shard_map(
        per_device, mesh=mesh, in_specs=in_specs, out_specs=out_specs, check_vma=False
    )
```

```python
import math

import jax
import jax.numpy as jnp
from jax import lax
from jax.sharding import PartitionSpec as P


def split_high(x):
    high = lax.reduce_precision(x, exponent_bits=8, mantissa_bits=7)
    low = x - high
    return jnp.concatenate([high.astype(jnp.bfloat16), low.astype(jnp.bfloat16)], axis=0)


def weighted_step(left, right, score):
    scaled = split_high(left.astype(jnp.float32) * score[:, None])
    both = jnp.concatenate([right, right], axis=0)
    return lax.dot_general(
        scaled, both, (((0,), (0,)), ((), ())), preferred_element_type=jnp.float32
    )


def per_device(
    token_ids,
    ranks,
    embed_table,
    norm_gain,
    gate_weight,
    up_weight,
    gate_left,
    up_left,
    gate_right,
    up_right,
):
    pops = lax.axis_size("pop")
    pop = lax.axis_index("pop")
    tensor = lax.axis_index("tensor")
    table_rows, features = embed_table.shape
    own_members, prompt = token_ids.shape
    row_count, hidden_cols = gate_weight.shape
    width = norm_gain.shape[0]
    members = own_members * pops
    part = -(-hidden_cols // (128 * pops)) * 128
    padded = part * pops

    own_tokens = own_members * prompt
    cap = 2 * own_tokens // pops

    def pad_cols(x):
        return jnp.pad(x, ((0, 0), (0, padded - hidden_cols)))

    def exchange(x):
        return lax.all_to_all(x, "pop", 0, 0, tiled=True)

    def spread(x):
        return exchange(jnp.broadcast_to(x[None], (pops,) + x.shape))

    shared = spread(jnp.concatenate([token_ids.reshape(-1), ranks]))
    all_ids = shared[:, :own_tokens]
    all_ranks = shared[:, own_tokens:].reshape(-1)

    earlier = (
        jnp.arange(own_tokens)[:, None] < jnp.arange(own_tokens)[None, :]
    ).astype(jnp.bfloat16)

    def place(owned):
        return jnp.dot(
            owned.astype(jnp.bfloat16), earlier, preferred_element_type=jnp.float32
        ).astype(jnp.int32)

    local_ids = all_ids - pop * table_rows
    owned = (local_ids >= 0) & (local_ids < table_rows)
    slot = jnp.where(owned, place(owned), -1)
    wanted = jnp.sum(
        jnp.where(slot[:, None, :] == jnp.arange(cap)[None, :, None], local_ids[:, None, :], 0),
        axis=-1,
    )
    rows = jnp.take(embed_table, wanted.reshape(-1), axis=0, mode="clip")
    factors = jnp.concatenate(
        [
            jnp.broadcast_to(
                jnp.concatenate([gate_right, up_right], axis=1)[None],
                (pops, own_members, 2 * hidden_cols),
            ),
            gate_left.reshape(own_members, pops, row_count).transpose(1, 0, 2),
            up_left.reshape(own_members, pops, row_count).transpose(1, 0, 2),
        ],
        axis=2,
    )
    factors, _ = lax.optimization_barrier((factors, shared))
    factors = exchange(factors)
    rows, factors = lax.optimization_barrier((rows, factors))
    arrived = exchange(rows)

    def transposed(weight):
        return lax.all_to_all(weight, "pop", 1, 0, tiled=True)

    def gather(x, axis):
        return lax.all_gather(x, axis, axis=int(axis == "tensor"), tiled=True)

    ids = token_ids.reshape(-1)
    owner = ids // table_rows
    mine_of = owner[None, :] == jnp.arange(pops)[:, None]
    rank_in = jnp.sum(jnp.where(mine_of, place(mine_of), 0), axis=0)
    source = owner * cap + rank_in
    pick = (source[:, None] == jnp.arange(pops * cap)[None, :]).astype(jnp.bfloat16)
    values = jnp.dot(pick, arrived, preferred_element_type=jnp.float32)

    total = lax.psum(jnp.sum(values * values, axis=-1), "tensor")
    gain = lax.dynamic_slice_in_dim(norm_gain, tensor * features, features, 0)
    own_normed = (
        values * lax.rsqrt(total[:, None] * (1.0 / width) + 1e-06) * gain.astype(jnp.float32)
    ).astype(jnp.bfloat16)

    def own_side(left):
        cols = lax.dynamic_slice_in_dim(left, tensor * features, features, 1)
        return jnp.sum(
            own_normed.astype(jnp.float32).reshape(own_members, prompt, features)
            * cols.astype(jnp.float32)[:, None, :],
            axis=-1,
        )

    scale = 0.5 / math.sqrt(width)
    sides = lax.psum(jnp.stack([own_side(gate_left), own_side(up_left)]), "tensor") * scale

    first = own_members * 5 // 8
    split = first * prompt
    gate_in, up_in = pad_cols(gate_weight), pad_cols(up_weight)
    own_normed, sides, gate_in, up_in = lax.optimization_barrier(
        (own_normed, sides, gate_in, up_in)
    )
    some1 = gather(own_normed[:split], "pop")
    gate_cols = transposed(gate_in)
    some1, gate_cols, up_in = lax.optimization_barrier((some1, gate_cols, up_in))
    normed1 = gather(some1, "tensor")
    up_cols = transposed(up_in)
    normed1, up_cols, own_rest, sides = lax.optimization_barrier(
        (normed1, up_cols, own_normed[split:], sides)
    )
    some2 = gather(own_rest, "pop")
    sides = spread(sides).reshape(pops, 2, own_members, prompt)
    factors = factors.reshape(members, 2 * (hidden_cols + row_count))
    all_gr = factors[:, :hidden_cols]
    all_ur = factors[:, hidden_cols : 2 * hidden_cols]
    left_gate = factors[:, 2 * hidden_cols : 2 * hidden_cols + row_count]
    left_up = factors[:, 2 * hidden_cols + row_count :]

    def right_cols(right):
        cols = lax.dynamic_slice_in_dim(pad_cols(right), pop * part, part, 1)
        return cols.astype(jnp.float32).reshape(pops, own_members, part)

    gate_right_cols = right_cols(all_gr)
    up_right_cols = right_cols(all_ur)

    def project(normed, weight, side, cols, lo, hi):
        base = jnp.dot(normed, weight, preferred_element_type=jnp.float32)
        return (
            base.reshape(pops, hi - lo, prompt, part)
            + side[:, lo:hi, :, None] * cols[:, lo:hi, None, :]
        )

    def activate(normed, lo, hi):
        gate = project(normed, gate_cols, sides[:, 0], gate_right_cols, lo, hi)
        up = project(normed, up_cols, sides[:, 1], up_right_cols, lo, hi)
        mine = (jax.nn.silu(gate) * up).astype(jnp.bfloat16)
        return mine.reshape(pops * (hi - lo) * prompt, part)

    def send_home(mine):
        return lax.all_to_all(mine, "pop", 0, 1, tiled=True)[:, :hidden_cols]

    mine1 = activate(normed1, 0, first)
    mine1, some2 = lax.optimization_barrier((mine1, some2))
    normed2 = gather(some2, "tensor")
    home1 = send_home(mine1)
    home2 = send_home(activate(normed2, first, own_members))
    pieces = [home1, home2]
    hidden = jnp.concatenate(pieces, axis=0)

    score = (2.0 * all_ranks.astype(jnp.float32) - (members - 1)) / (members - 1)
    score = score * (1.0 / math.sqrt(members))
    gate_step = weighted_step(left_gate, all_gr, score)
    up_step = weighted_step(left_up, all_ur, score)
    return (hidden, gate_step, up_step)


def solution(mesh):
    in_specs = (
        P("pop", None),
        P("pop"),
        P("pop", "tensor"),
        P(),
        P("pop", "tensor"),
        P("pop", "tensor"),
        P("pop", None),
        P("pop", None),
        P("pop", "tensor"),
        P("pop", "tensor"),
    )
    out_specs = (P("pop", "tensor"), P("pop", "tensor"), P("pop", "tensor"))
    return jax.shard_map(
        per_device, mesh=mesh, in_specs=in_specs, out_specs=out_specs, check_vma=False
    )
```
